256 devices in a mesh: gz: 4 (over y), row: 8 (over x, core), col: 8 (over z).
Axes of the slice: x: 4, y: 4, z: 8, core: 2. Of those that a mesh axis runs over, the one named last changes fastest.
Arguments:
- front_in: bfloat16 [4, 16384, 8192], P('gz', 'row', 'col'), may hold values from -6 to 6
- pattern: int32 [4, 64, 32], P('gz', 'row', 'col'), may hold values 0 or 1
- lower_inv: float32 [4, 2, 256, 256], P('gz'), as said below
- upper_inv: float32 [4, 2, 256, 256], P('gz'), as said below
- targets: int32 [4, 16384], P('gz', 'row'), may hold values from 0 to 65535, as said below
Outputs:
- lower_fac: bfloat16 [4, 16384, 512], P('gz', 'row')
- upper_fac: bfloat16 [4, 512, 8192], P('gz', None, 'col')
- ancestor: float32 [65536, 8192], P(('gz', 'row'), 'col')
The draws below stay inside these ranges and needn't reach their ends.
Inputs may be any that keep to these rules, and one draw needn't show every extreme that they name: Within one group the targets of rows 512 and beyond are distinct. Take the ancestor rows in shards of 2048 rows, shard p holding rows p * 8 * 256 onward: among the 2048 rows of a group that one index of row holds, at most 96 have targets in one shard, and exactly 96 in half of the shards. lower_inv[g, k] is lower triangular with a positive diagonal. upper_inv[g, k] is upper triangular with a positive diagonal.
All inputs are finite; a program needn't handle non-finite values. No bound on the sum of `pattern` on one device may be relied on, other than what follows from the above.
Results may differ from the reference program's by a relative error of at most 0.0032.
Values may be sent and summed in bfloat16 or wider, within the bound.
No kernel may reach another device: no remote copies, remote signals or barrier semaphores. Data moves between devices by JAX's collectives and lax.ppermute only.
A program may use at most 128 MiB of HBM per device.

```python
import math
import jax
import jax.numpy as jnp
from jax import lax

B = 256
R = 8
NBR = 64
NBC = 32
NFR = 16384
NFC = 8192
NANC = 65536
CAP = 96
N_GZ = 4
N_ROW = 8


def make_inverse(key, below):
    diag_key, off_key = jax.random.split(key)
    index_rows = jnp.arange(B)[:, None]
    index_cols = jnp.arange(B)[None, :]
    diagonal_part = jax.random.uniform(diag_key, (N_GZ, 2, B), jnp.float32, 0.5, 1.5) * 0.125
    off_part = jax.random.uniform(off_key, (N_GZ, 2, B, B), jnp.float32, -1.0, 1.0) * (0.2 / math.sqrt(B))
    if below:
        side_mask = index_rows > index_cols
    else:
        side_mask = index_rows < index_cols
    on_diag = index_rows == index_cols
    return jnp.where(side_mask, off_part, 0.0) + jnp.where(on_diag, diagonal_part[..., :, None], 0.0)


def draw_lower_inv(key, part):
    key = jax.random.fold_in(key, 11)
    return make_inverse(key, True)


def draw_upper_inv(key, part):
    key = jax.random.fold_in(key, 23)
    return make_inverse(key, False)


def draw_targets(key, part):
    key = jax.random.fold_in(key, 37)
    peer_count = N_GZ * N_ROW
    rows_dev = R * B
    light_count = rows_dev // (2 * peer_count)
    half_peers = peer_count // 2
    peer_key, slot_key = jax.random.split(key)
    position = jnp.arange(rows_dev)
    label_index = jnp.where(position < half_peers * CAP, position // CAP, half_peers + (position - half_peers * CAP) // light_count)

    def device_labels(device_key):
        first_key, second_key = jax.random.split(device_key)
        order = jax.random.permutation(first_key, peer_count)
        labels = order[label_index]
        return labels[jax.random.permutation(second_key, rows_dev)]
    peers = jax.vmap(device_labels)(jax.random.split(peer_key, N_GZ * N_ROW)).reshape(N_GZ, N_ROW * rows_dev)
    one_hot = (peers[:, :, None] == jnp.arange(peer_count)[None, None, :]).astype(jnp.int32)
    running = jnp.cumsum(one_hot, axis=1) - 1
    slot_rank = jnp.sum(one_hot * running, axis=2)
    slot_perms = jax.vmap(lambda inner_key: jax.random.permutation(inner_key, rows_dev))(jax.random.split(slot_key, N_GZ * peer_count)).reshape(N_GZ, peer_count, rows_dev)
    group_ids = jnp.arange(N_GZ)[:, None]
    local_rows = slot_perms[group_ids, peers, slot_rank]
    return (peers * rows_dev + local_rows).astype(jnp.int32)


def place_ends(array, own_key, smallest, largest):
    longest = array.shape.index(max(array.shape))
    spots = []
    for shift in (0, 1):
        where = [jax.random.randint(jax.random.fold_in(own_key, axis), (), 0, length) for axis, length in enumerate(array.shape)]
        where[longest] = (where[longest] + shift) % array.shape[longest]
        spots.append(tuple(where))
    return array.at[spots[0]].set(smallest).at[spots[1]].set(largest)


def levels(key, dims, cuts, least, largest):
    level = 1.0
    for axis_at, blocks in cuts:
        heights = jax.random.uniform(jax.random.fold_in(jax.random.fold_in(key, 6), axis_at), (blocks,), jnp.float32, least / len(cuts), largest / len(cuts))
        level = level * jnp.repeat(jnp.exp(heights), dims[axis_at] // blocks).reshape((-1,) + (1,) * (len(dims) - 1 - axis_at))
    return level


def noise(rng, dims, deviation, limit, shards=(), held_as=jnp.bfloat16):
    result = deviation * jax.random.normal(rng, dims, jnp.float32)
    if shards:
        result = result * levels(rng, dims, shards, -0.22, 0.18)
    return jnp.clip(result, -limit, limit).astype(held_as)


def setup_inputs(seed: int = 0) -> dict:
    seeds = jax.random.split(jax.random.key(seed), 6)
    front_in = noise(seeds[0], (N_GZ, NFR, NFC), 1.0, 6.0, ((0, 4), (1, 8), (2, 8)))
    pattern = place_ends((jax.random.randint(seeds[1], (N_GZ, NBR, NBC), 0, 4) < 3).astype(jnp.int32), jax.random.fold_in(seeds[1], 1), 0, 1)
    lower_inv = draw_lower_inv(jax.random.fold_in(seeds[5], 71), 0)
    upper_inv = draw_upper_inv(jax.random.fold_in(seeds[5], 71), 0)
    targets = draw_targets(jax.random.fold_in(seeds[5], 71), 0)
    return {"front_in": front_in, "pattern": pattern, "lower_inv": lower_inv, "upper_inv": upper_inv, "targets": targets}


def expand(matrix, pattern_f, block_size):
    rows_n, cols_n = matrix.shape
    shaped = matrix.reshape(rows_n // block_size, block_size, cols_n // block_size, block_size)
    return (shaped * pattern_f[:, None, :, None]).reshape(rows_n, cols_n)


def reference(front_in, pattern, lower_inv, upper_inv, targets):
    highest = lax.Precision.HIGHEST
    ancestor = jnp.zeros((NANC, NFC), jnp.float32)
    row_block = jnp.arange(NFR) // B
    col_block = jnp.arange(NFC) // B
    lower_list = []
    upper_list = []
    for group_id in range(N_GZ):
        pattern_f = pattern[group_id].astype(jnp.float32)
        matrix = expand(front_in[group_id].astype(jnp.float32), pattern_f, B)
        lower_parts = []
        upper_parts = []
        for step_level in range(2):
            lower_panel = jnp.dot(matrix[:, step_level * B:(step_level + 1) * B], upper_inv[group_id, step_level], precision=highest, preferred_element_type=jnp.float32)
            lower_panel = jnp.where((row_block > step_level)[:, None], lower_panel, jnp.float32(0.0)).astype(jnp.bfloat16)
            upper_panel = jnp.dot(lower_inv[group_id, step_level], matrix[step_level * B:(step_level + 1) * B, :], precision=highest, preferred_element_type=jnp.float32)
            upper_panel = jnp.where((col_block > step_level)[None, :], upper_panel, jnp.float32(0.0)).astype(jnp.bfloat16)
            product = jnp.dot(lower_panel, upper_panel, preferred_element_type=jnp.float32)
            matrix = matrix - expand(product, pattern_f, B)
            lower_parts.append(lower_panel)
            upper_parts.append(upper_panel)
        keep_mask = (row_block >= 2)[:, None] & (col_block >= 2)[None, :]
        contribution = jnp.where(keep_mask, matrix, jnp.float32(0.0)).astype(jnp.bfloat16)
        ancestor = ancestor.at[targets[group_id, 2 * B:]].add(contribution[2 * B:].astype(jnp.float32))
        lower_list.append(jnp.concatenate(lower_parts, axis=1))
        upper_list.append(jnp.concatenate(upper_parts, axis=0))
    return jnp.stack(lower_list), jnp.stack(upper_list), ancestor
```

```python
import jax
import jax.numpy as jnp
from jax import lax
from jax.experimental import pallas as pl
from jax.experimental.pallas import tpu as pltpu
from jax.sharding import PartitionSpec as P

BF = jnp.bfloat16
F32 = jnp.float32
B = 256
CAP = 96
VMEM_LIMIT = 48 * 2**20


def params():
    return pltpu.CompilerParams(vmem_limit_bytes=VMEM_LIMIT)


def mm(a, b):
    return jnp.dot(a, b, preferred_element_type=F32)


def split(a):
    hi = a.astype(BF)
    return hi, (a - hi.astype(F32)).astype(BF)


def dot_split(a, b):
    ah, al = split(a)
    bh, bl = split(b)
    return mm(ah, bh) + (mm(ah, bl) + mm(al, bh))


def panels_zero_kernel(pos_ref, pat_ref, cols_ref, rows_ref, li_ref, ui_ref, l_ref, u_ref):
    n_row, n_col = l_ref.shape[0] // B, u_ref.shape[1] // B
    row0, col0 = pos_ref[0] * n_row, pos_ref[1] * n_col
    uh, ul = split(ui_ref[0, 0])
    lh, ll = split(li_ref[0, 0])
    for i in range(n_row):
        keep = jnp.where(row0 + i > 0, pat_ref[i, 0], 0).astype(F32)
        block = cols_ref[0, i * B : (i + 1) * B, 0:B]
        l_ref[i * B : (i + 1) * B, :] = ((mm(block, uh) + mm(block, ul)) * keep).astype(BF)
    for j in range(n_col):
        keep = jnp.where(col0 + j > 0, pat_ref[0, j], 0).astype(F32)
        block = rows_ref[0, 0:B, j * B : (j + 1) * B]
        u_ref[:, j * B : (j + 1) * B] = ((mm(lh, block) + mm(ll, block)) * keep).astype(BF)


def panels_one_kernel(
    pos_ref, pat_ref, cols_ref, rows_ref, li_ref, ui_ref, l0_ref, u0_ref, uc_ref, lc_ref, l_ref, u_ref
):
    n_row, n_col = l_ref.shape[0] // B, u_ref.shape[1] // B
    row0, col0 = pos_ref[0] * n_row, pos_ref[1] * n_col
    ui, li = ui_ref[0, 1], li_ref[0, 1]
    for i in range(n_row):
        keep = jnp.where(row0 + i > 1, pat_ref[i, 1], 0).astype(F32)
        rows = slice(i * B, (i + 1) * B)
        block = cols_ref[0, rows, B : 2 * B].astype(F32) - mm(l0_ref[rows, :], uc_ref[...])
        l_ref[rows, :] = (dot_split(block, ui) * keep).astype(BF)
    for j in range(n_col):
        keep = jnp.where(col0 + j > 1, pat_ref[1, j], 0).astype(F32)
        cols = slice(j * B, (j + 1) * B)
        block = rows_ref[0, B : 2 * B, cols].astype(F32) - mm(lc_ref[...], u0_ref[:, cols])
        u_ref[:, cols] = (dot_split(li, block) * keep).astype(BF)


def slots_kernel(pos_ref, targets_ref, slot_ref, value_ref):
    rows = targets_ref.shape[1]
    peers = 32
    target = targets_ref[...]
    peer = target // rows
    local = target - peer * rows
    row_id = pos_ref[0] * rows + lax.broadcasted_iota(jnp.int32, (1, rows), 1)
    valid = row_id >= 2 * B
    ids = lax.broadcasted_iota(jnp.int32, (peers, rows), 0)
    hot = jnp.where((ids == peer) & valid, 1.0, 0.0)
    before = jnp.where(
        lax.broadcasted_iota(jnp.int32, (B, B), 0) < lax.broadcasted_iota(jnp.int32, (B, B), 1), 1.0, 0.0
    ).astype(BF)
    seen = jnp.zeros((peers, 1), F32)
    for i in range(rows // B):
        part = hot[:, i * B : (i + 1) * B]
        rank = mm(part.astype(BF), before) + seen
        seen = seen + jnp.sum(part, axis=1, keepdims=True)
        place = rank + (CAP * ids[:, i * B : (i + 1) * B]).astype(F32)
        slot = jnp.sum(part * place, axis=0, keepdims=True).astype(jnp.int32)
        ok = valid[:, i * B : (i + 1) * B]
        slot_ref[:, i * B : (i + 1) * B] = jnp.where(ok, slot, -1)
    high = local // 64
    which = lax.broadcasted_iota(jnp.int32, (16, rows), 0)
    value = jnp.where(which == 0, high, jnp.where(which == 1, local - high * 64, jnp.where(which == 2, 1, 0)))
    value_ref[...] = value.astype(F32).astype(BF)


def one_hot(first, count, slot):
    ids = first + lax.broadcasted_iota(jnp.int32, (count, slot.shape[1]), 0)
    return jnp.where(ids == slot, 1.0, 0.0).astype(BF)


def pack_kernel(slot_ref, value_ref, front_ref, pat_ref, rows_ref, keep_ref, index_ref):
    count = rows_ref.shape[0]
    hot = one_hot(pl.program_id(0) * count, count, slot_ref[...])
    keep = mm(hot, pat_ref[...])
    keep_ref[...] = keep.astype(BF)
    for j in range(rows_ref.shape[1] // B):
        cols = slice(j * B, (j + 1) * B)
        rows_ref[:, cols] = (mm(hot, front_ref[0, :, cols]) * keep[:, j : j + 1]).astype(BF)
    info = lax.dot_general(value_ref[...], hot, (((1,), (1,)), ((), ())), preferred_element_type=F32)
    index = info[0:1] * 64.0 + info[1:2] + (1.0 - info[2:3]) * 4096.0
    index_ref[...] = jnp.broadcast_to(index, (8, count)).astype(jnp.int32)


def update_kernel(slot_ref, lower_ref, u0_ref, u1_ref, rows_ref, keep_ref, out_ref):
    count = rows_ref.shape[0]
    hot = one_hot(pl.program_id(0) * count, count, slot_ref[...])
    low = mm(hot, lower_ref[...]).astype(BF)
    for j in range(rows_ref.shape[1] // B):
        cols = slice(j * B, (j + 1) * B)
        product = mm(low[:, 0:B], u0_ref[:, cols]) + mm(low[:, B : 2 * B], u1_ref[:, cols])
        keep = keep_ref[:, j : j + 1].astype(F32)
        out_ref[:, cols] = (rows_ref[:, cols].astype(F32) - product * keep).astype(BF)


def add_kernel(index_ref, got_ref, out_ref):
    hot = one_hot(pl.program_id(0) * out_ref.shape[0], out_ref.shape[0], index_ref[...])
    out_ref[...] = mm(hot, got_ref[...])


def whole(shape):
    return pl.BlockSpec(shape, lambda *_: (0,) * len(shape))


SMEM = pl.BlockSpec(memory_space=pltpu.SMEM)
TREE = (((0, 4),), ((0, 2), (4, 6)), ((0, 1), (2, 3), (4, 5), (6, 7)))


def tree(block, axis):
    block = jnp.where(lax.axis_index(axis) == 0, block, jnp.zeros_like(block))
    for pairs in TREE:
        block = block + lax.ppermute(block, axis, pairs)
    return block


def spread(lower, axis):
    n = lax.axis_size(axis)
    rows = lower.shape[0] // n
    piece = jnp.where(lax.axis_index(axis) == 0, lower[:rows], jnp.zeros_like(lower[:rows]))
    for c in range(1, n):
        piece = piece + lax.ppermute(lower[c * rows : (c + 1) * rows], axis, [(0, c)])
    return lax.all_gather(piece, axis, axis=0, tiled=True)


def local(front_in, pattern, lower_inv, upper_inv, targets):
    rows, width = front_in.shape[1:]
    n_col = width // B
    peers = lax.axis_size("gz") * lax.axis_size("row")
    slots = peers * CAP
    pos = jnp.stack([lax.axis_index("row"), lax.axis_index("col")]).astype(jnp.int32)
    pat = pattern[0]
    part = slots // 4

    cols_spec = pl.BlockSpec((1, rows, 2 * B), lambda *_: (0, 0, 0))
    rows_spec = pl.BlockSpec((1, 2 * B, width), lambda *_: (0, 0, 0))
    inv_spec = whole((1, 2, B, B))
    shapes = (jax.ShapeDtypeStruct((rows, B), BF), jax.ShapeDtypeStruct((B, width), BF))
    l0, u0 = pl.pallas_call(
        panels_zero_kernel,
        grid=(1,),
        in_specs=[SMEM, SMEM, cols_spec, rows_spec, inv_spec, inv_spec],
        out_specs=[whole((rows, B)), whole((B, width))],
        out_shape=shapes,
        compiler_params=params(),
        name="panels_zero",
    )(pos, pat, front_in, front_in, lower_inv, upper_inv)
    upper_corner = tree(u0[:, B : 2 * B], "row")
    lower_corner = tree(l0[B : 2 * B], "col")
    l1, u1 = pl.pallas_call(
        panels_one_kernel,
        grid=(1,),
        in_specs=[SMEM, SMEM, cols_spec, rows_spec, inv_spec, inv_spec]
        + [whole((rows, B)), whole((B, width)), whole((B, B)), whole((B, B))],
        out_specs=[whole((rows, B)), whole((B, width))],
        out_shape=shapes,
        compiler_params=params(),
        name="panels_one",
    )(pos, pat, front_in, front_in, lower_inv, upper_inv, l0, u0, upper_corner, lower_corner)

    slot, value = pl.pallas_call(
        slots_kernel,
        in_specs=[SMEM, pl.BlockSpec(memory_space=pltpu.VMEM)],
        out_shape=(jax.ShapeDtypeStruct((1, rows), jnp.int32), jax.ShapeDtypeStruct((16, rows), BF)),
        name="slots",
    )(pos, targets)
    keep_col = (pos[1] * n_col + jnp.arange(n_col)) >= 2
    keep_pat = jnp.where(keep_col[None, :], pat, 0).astype(BF)
    pat_rows = jnp.pad(jnp.repeat(keep_pat, B, axis=0), ((0, 0), (0, 128 - n_col)))
    packed, keep, index = pl.pallas_call(
        pack_kernel,
        grid=(4,),
        in_specs=[whole((1, rows)), whole((16, rows)), whole((1, rows, width)), whole((rows, 128))],
        out_specs=[
            pl.BlockSpec((part, width), lambda i: (i, 0)),
            pl.BlockSpec((part, 128), lambda i: (i, 0)),
            pl.BlockSpec((8, part), lambda i: (0, i)),
        ],
        out_shape=(
            jax.ShapeDtypeStruct((slots, width), BF),
            jax.ShapeDtypeStruct((slots, 128), BF),
            jax.ShapeDtypeStruct((8, slots), jnp.int32),
        ),
        compiler_params=params(),
        name="pack",
    )(slot, value, front_in, pat_rows)
    got_index = lax.all_to_all(
        index[0].reshape(peers, CAP), ("gz", "row"), split_axis=0, concat_axis=0, tiled=True
    ).reshape(1, slots)

    upper_zero = tree(u0, "row")
    upper_one = tree(u1, "row")
    lower = spread(jnp.concatenate([l0, l1], axis=1), "col")

    send = pl.pallas_call(
        update_kernel,
        grid=(4,),
        in_specs=[
            whole((1, rows)),
            whole((rows, 2 * B)),
            whole((B, width)),
            whole((B, width)),
            pl.BlockSpec((part, width), lambda i: (i, 0)),
            pl.BlockSpec((part, 128), lambda i: (i, 0)),
        ],
        out_specs=pl.BlockSpec((part, width), lambda i: (i, 0)),
        out_shape=jax.ShapeDtypeStruct((slots, width), BF),
        compiler_params=params(),
        name="update",
    )(slot, lower, upper_zero, upper_one, packed, keep)
    got = lax.all_to_all(
        send.reshape(peers, CAP, width), ("gz", "row"), split_axis=0, concat_axis=0, tiled=True
    ).reshape(slots, width)
    ancestor = pl.pallas_call(
        add_kernel,
        grid=(8,),
        in_specs=[whole((1, slots)), whole((slots, width))],
        out_specs=pl.BlockSpec((rows // 8, width), lambda i: (i, 0)),
        out_shape=jax.ShapeDtypeStruct((rows, width), F32),
        compiler_params=params(),
        name="add",
    )(got_index, got)
    upper = jnp.concatenate([upper_zero, upper_one], axis=0)[None]
    return (lower[None], upper, ancestor)


def solution(mesh):
    return jax.shard_map(
        local,
        mesh=mesh,
        in_specs=(
            P("gz", "row", "col"),
            P("gz", "row", "col"),
            P("gz", None, None, None),
            P("gz", None, None, None),
            P("gz", "row"),
        ),
        out_specs=(P("gz", "row", None), P("gz", None, "col"), P(("gz", "row"), "col")),
        check_vma=False,
    )
```

```python
import jax
import jax.numpy as jnp
from jax import lax
from jax.experimental import pallas as pl
from jax.experimental.pallas import tpu as pltpu
from jax.sharding import PartitionSpec as P

BF = jnp.bfloat16
F32 = jnp.float32
B = 256
CAP = 96
NOTE = 16
VMEM_LIMIT = 48 * 2**20


def params():
    return pltpu.CompilerParams(vmem_limit_bytes=VMEM_LIMIT)


def mm(a, b):
    return jnp.dot(a, b, preferred_element_type=F32)


def split(a):
    hi = a.astype(BF)
    return hi, (a - hi.astype(F32)).astype(BF)


def dot_split(a, b):
    ah, al = split(a)
    bh, bl = split(b)
    return mm(ah, bh) + (mm(ah, bl) + mm(al, bh))


def panels_zero_kernel(
    pos_ref, pat_ref, cols_ref, rows_ref, li_ref, ui_ref, send_ref, u_ref, corner_ref
):
    n_row, n_col = cols_ref.shape[1] // B, u_ref.shape[1] // B
    row0, col0 = pos_ref[0] * n_row, pos_ref[1] * n_col
    uh, ul = split(ui_ref[0, 0])
    lh, ll = split(li_ref[0, 0])
    for i in range(n_row):
        keep = jnp.where(row0 + i > 0, pat_ref[i, 0], 0).astype(F32)
        second = pat_ref[i, 1].astype(F32)
        block = cols_ref[0, i * B : (i + 1) * B, 0:B]
        base = i * (B + NOTE)
        send_ref[base : base + B, 0:B] = ((mm(block, uh) + mm(block, ul)) * keep).astype(BF)
        block = cols_ref[0, i * B : (i + 1) * B, B : 2 * B].astype(F32)
        send_ref[base : base + B, B : 2 * B] = (block * second).astype(BF)
        send_ref[base + B : base + B + NOTE, :] = (jnp.zeros((NOTE, 2 * B), F32) + second).astype(BF)
    for j in range(n_col):
        keep = jnp.where(col0 + j > 0, pat_ref[0, j], 0).astype(F32)
        block = rows_ref[0, 0:B, j * B : (j + 1) * B]
        u_ref[:, j * B : (j + 1) * B] = ((mm(lh, block) + mm(ll, block)) * keep).astype(BF)
    root = (pos_ref[1] == 0).astype(F32)
    corner_ref[0:B, :] = (send_ref[B + NOTE : 2 * B + NOTE, 0:B].astype(F32) * root).astype(BF)
    corner_ref[B : 2 * B, :] = (u_ref[:, B : 2 * B].astype(F32) * root).astype(BF)


def upper_kernel(pos_ref, pat_ref, rows_ref, li_ref, u0_ref, corner_ref, out_ref):
    n_col = u0_ref.shape[1] // B
    col0 = pos_ref[1] * n_col
    root = (pos_ref[0] == 0).astype(F32)
    out_ref[0:B, :] = (u0_ref[...].astype(F32) * root).astype(BF)
    n = B // n_col
    for j in range(n_col):
        keep = jnp.where(col0 + j > 1, pat_ref[1, j], 0).astype(F32)
        cols = slice(j * B, (j + 1) * B)
        block = rows_ref[0, B : 2 * B, cols].astype(F32) - mm(corner_ref[0:B, :], u0_ref[:, cols])
        out_ref[B : 2 * B, cols] = (dot_split(li_ref[0, 1], block) * (keep * root)).astype(BF)
        piece = corner_ref[B + j * n : B + (j + 1) * n, :].astype(F32)
        out_ref[2 * B : 2 * B + n, cols] = (piece * root).astype(BF)


def slots_kernel(pos_ref, targets_ref, slot_ref, value_ref):
    rows = targets_ref.shape[1]
    peers = 32
    target = targets_ref[...]
    peer = target // rows
    local = target - peer * rows
    row_id = pos_ref[0] * rows + lax.broadcasted_iota(jnp.int32, (1, rows), 1)
    valid = row_id >= 2 * B
    ids = lax.broadcasted_iota(jnp.int32, (peers, rows), 0)
    hot = jnp.where((ids == peer) & valid, 1.0, 0.0)
    before = jnp.where(
        lax.broadcasted_iota(jnp.int32, (B, B), 0) < lax.broadcasted_iota(jnp.int32, (B, B), 1), 1.0, 0.0
    ).astype(BF)
    seen = jnp.zeros((peers, 1), F32)
    for i in range(rows // B):
        part = hot[:, i * B : (i + 1) * B]
        rank = mm(part.astype(BF), before) + seen
        seen = seen + jnp.sum(part, axis=1, keepdims=True)
        place = rank + (CAP * ids[:, i * B : (i + 1) * B]).astype(F32)
        slot = jnp.sum(part * place, axis=0, keepdims=True).astype(jnp.int32)
        ok = valid[:, i * B : (i + 1) * B]
        slot_ref[:, i * B : (i + 1) * B] = jnp.where(ok, slot, -1)
    high = local // 64
    which = lax.broadcasted_iota(jnp.int32, (16, rows), 0)
    value = jnp.where(which == 0, high, jnp.where(which == 1, local - high * 64, jnp.where(which == 2, 1, 0)))
    value_ref[...] = value.astype(F32).astype(BF)


def one_hot(first, count, slot):
    ids = first + lax.broadcasted_iota(jnp.int32, (count, slot.shape[1]), 0)
    return jnp.where(ids == slot, 1.0, 0.0).astype(BF)


def pack_rows(first, hot, front_ref, keep, rows_ref):
    for j in range(rows_ref.shape[1] // B):
        cols = slice(j * B, (j + 1) * B)
        rows_ref[:, cols] = (mm(hot, front_ref[0, :, cols]) * keep[:, first + j : first + j + 1]).astype(BF)


def pack_head_kernel(first, slot_ref, value_ref, front_ref, pat_ref, *refs):
    rows_ref, keep_ref, index_ref = refs[-3:]
    count = rows_ref.shape[0]
    hot = one_hot((first + pl.program_id(0)) * count, count, slot_ref[...])
    keep = mm(hot, pat_ref[...])
    keep_ref[...] = keep.astype(BF)
    pack_rows(0, hot, front_ref, keep, rows_ref)
    info = lax.dot_general(value_ref[...], hot, (((1,), (1,)), ((), ())), preferred_element_type=F32)
    index = info[0:1] * 64.0 + info[1:2] + (1.0 - info[2:3]) * 4096.0
    index_ref[...] = jnp.broadcast_to(index, (8, count)).astype(jnp.int32)


def pack_tail_kernel(first, slot_ref, front_ref, keep_ref, after_ref, rows_ref):
    count = rows_ref.shape[0]
    hot = one_hot(pl.program_id(0) * count, count, slot_ref[...])
    pack_rows(first, hot, front_ref, keep_ref[...].astype(F32), rows_ref)


def subtract(out_ref, rows_ref, keep_ref, first, low, u_ref):
    for j in range(out_ref.shape[1] // B):
        cols = slice(j * B, (j + 1) * B)
        product = mm(low, u_ref[0 : 2 * B, cols])
        keep = keep_ref[:, first + j : first + j + 1].astype(F32)
        out_ref[:, cols] = (rows_ref[:, cols].astype(F32) - product * keep).astype(BF)


def update_kernel(
    pos_ref, slot_ref, all_ref, ui_ref, u_ref, rows_ref, keep_ref, out_ref, low_ref, lower_ref
):
    n_row = lower_ref.shape[0] // B
    n_col = u_ref.shape[1] // B

    @pl.when(pl.program_id(0) == 0)
    def _():
        corner = jnp.concatenate([u_ref[2 * B :, j * B : (j + 1) * B] for j in range(n_col)], axis=0)
        uh, ul = split(ui_ref[0, 1])
        for i in range(n_row):
            base, rows = i * (B + NOTE), slice(i * B, (i + 1) * B)
            low = all_ref[base : base + B, 0:B]
            keep = all_ref[base + B : base + B + NOTE, B : 2 * B].astype(F32)[0:1]
            keep = keep * (pos_ref[0] * n_row + i > 1).astype(F32)
            block = all_ref[base : base + B, B : 2 * B].astype(F32) - mm(low, corner)
            bh, bl = split(block)
            lower_ref[rows, 0:B] = low
            lower_ref[rows, B : 2 * B] = ((mm(bh, uh) + (mm(bh, ul) + mm(bl, uh))) * keep).astype(BF)

    count = rows_ref.shape[0]
    hot = one_hot(pl.program_id(0) * count, count, slot_ref[...])
    low = mm(hot, lower_ref[...]).astype(BF)
    low_ref[...] = low
    subtract(out_ref, rows_ref, keep_ref, 0, low, u_ref)


def rest_kernel(first, low_ref, u_ref, rows_ref, keep_ref, out_ref):
    subtract(out_ref, rows_ref, keep_ref, first, low_ref[...], u_ref)


def join_kernel(pos_ref, own_ref, *refs):
    piece_ref = refs[-1]
    piece = own_ref[...].astype(F32) * (pos_ref[1] == 0).astype(F32)
    for ref in refs[:-1]:
        piece = piece + ref[...].astype(F32)
    piece_ref[...] = piece.astype(BF)


def add_kernel(index_ref, got_ref, *refs):
    out_ref = refs[-1]
    hot = one_hot(pl.program_id(0) * out_ref.shape[0], out_ref.shape[0], index_ref[...])
    out_ref[...] = mm(hot, got_ref[...])


def cost(flops, size):
    return pl.CostEstimate(flops=flops, bytes_accessed=size, transcendentals=0)


def whole(shape):
    return pl.BlockSpec(shape, lambda *_: (0,) * len(shape))


SMEM = pl.BlockSpec(memory_space=pltpu.SMEM)
ANY = pl.BlockSpec(memory_space=pl.ANY)
TREE = (((0, 4),), ((0, 2), (4, 6)), ((0, 1), (2, 3), (4, 5), (6, 7)))


def tree(block, axis):
    for pairs in TREE:
        block = block + lax.ppermute(block, axis, pairs)
    return block


def sum_kernel(a_ref, b_ref, *refs):
    refs[-1][...] = (a_ref[...].astype(F32) + b_ref[...].astype(F32)).astype(BF)


def plus(a, b, *after):
    return pl.pallas_call(
        sum_kernel,
        grid=(1,),
        in_specs=[whole(a.shape)] * 2 + [ANY] * len(after),
        out_specs=whole(a.shape),
        out_shape=jax.ShapeDtypeStruct(a.shape, a.dtype),
        compiler_params=params(),
        cost_estimate=cost(0, 6 * a.size),
        name="plus",
    )(a, b, *after)


def scatter(lower, axis, pos):
    n = lax.axis_size(axis)
    rows = lower.shape[0] // n
    shape = (rows, lower.shape[1])
    got = [lax.ppermute(lower[c * rows : (c + 1) * rows], axis, [(0, c)]) for c in range(1, n)]
    return pl.pallas_call(
        join_kernel,
        grid=(1,),
        in_specs=[SMEM] + [whole(shape)] * n,
        out_specs=whole(shape),
        out_shape=jax.ShapeDtypeStruct(shape, lower.dtype),
        compiler_params=params(),
        cost_estimate=cost(0, 18 * rows * lower.shape[1]),
        name="join",
    )(pos, lower, *got)


def local(front_in, pattern, lower_inv, upper_inv, targets):
    rows, width = front_in.shape[1:]
    n_row, n_col = rows // B, width // B
    peers = lax.axis_size("gz") * lax.axis_size("row")
    slots = peers * CAP
    pos = jnp.stack([lax.axis_index("row"), lax.axis_index("col")]).astype(jnp.int32)
    pat = pattern[0]
    part = slots // 4
    head = 3 * width // 4
    tail = width - head
    last = head // tail
    exchange = lambda x: lax.all_to_all(x, ("gz", "row"), split_axis=0, concat_axis=0, tiled=True)

    slot, value = pl.pallas_call(
        slots_kernel,
        in_specs=[SMEM, pl.BlockSpec(memory_space=pltpu.VMEM)],
        out_shape=(jax.ShapeDtypeStruct((1, rows), jnp.int32), jax.ShapeDtypeStruct((16, rows), BF)),
        cost_estimate=cost(10**9, 10**6),
        name="slots",
    )(pos, targets)

    cols_spec = pl.BlockSpec((1, rows, 2 * B), lambda *_: (0, 0, 0))
    rows_spec = pl.BlockSpec((1, 2 * B, width), lambda *_: (0, 0, 0))
    inv_spec = whole((1, 2, B, B))
    sent = n_row * (B + NOTE)
    upper_rows = 2 * B + B // n_col
    send, u0, corner = pl.pallas_call(
        panels_zero_kernel,
        grid=(1,),
        in_specs=[SMEM, SMEM, cols_spec, rows_spec, inv_spec, inv_spec],
        out_specs=[whole((sent, 2 * B)), whole((B, width)), whole((2 * B, B))],
        out_shape=(
            jax.ShapeDtypeStruct((sent, 2 * B), BF),
            jax.ShapeDtypeStruct((B, width), BF),
            jax.ShapeDtypeStruct((2 * B, B), BF),
        ),
        compiler_params=params(),
        cost_estimate=cost(4 * (rows + width) * B * B, 8 * (rows + width) * B),
        name="panels_zero",
    )(pos, pat, front_in, front_in, lower_inv, upper_inv)
    piece = scatter(send, "col", pos)
    everything = lax.all_gather(piece, "col", axis=0, tiled=True)
    corner = tree(corner, "col")
    upper = pl.pallas_call(
        upper_kernel,
        grid=(1,),
        in_specs=[SMEM, SMEM, rows_spec, inv_spec, whole((B, width)), whole((2 * B, B))],
        out_specs=whole((upper_rows, width)),
        out_shape=jax.ShapeDtypeStruct((upper_rows, width), BF),
        compiler_params=params(),
        cost_estimate=cost(8 * width * B * B, 8 * width * B),
        name="upper",
    )(pos, pat, front_in, lower_inv, u0, corner)

    keep_col = (pos[1] * n_col + jnp.arange(n_col)) >= 2
    keep_pat = jnp.where(keep_col[None, :], pat, 0).astype(BF)
    pat_rows = jnp.pad(jnp.repeat(keep_pat, B, axis=0), ((0, 0), (0, 128 - n_col)))
    keep_spec = pl.BlockSpec((part, 128), lambda i: (i, 0))
    head_spec = pl.BlockSpec((part, head), lambda i: (i, 0))
    tail_spec = pl.BlockSpec((part, tail), lambda i: (i, 0))
    low_spec = pl.BlockSpec((part, 2 * B), lambda i: (i, 0))
    shapes = (
        jax.ShapeDtypeStruct((slots, head), BF),
        jax.ShapeDtypeStruct((slots, 128), BF),
        jax.ShapeDtypeStruct((8, slots), jnp.int32),
    )

    def pack_head(first, after, made):
        return pl.pallas_call(
            lambda *refs: pack_head_kernel(first, *refs),
            grid=(2,),
            in_specs=[
                whole((1, rows)),
                whole((16, rows)),
                pl.BlockSpec((1, rows, head), lambda i: (0, 0, 0)),
                whole((rows, 128)),
            ]
            + [ANY] * (1 + len(made)),
            out_specs=[
                pl.BlockSpec((part, head), lambda i: (first + i, 0)),
                pl.BlockSpec((part, 128), lambda i: (first + i, 0)),
                pl.BlockSpec((8, part), lambda i: (0, first + i)),
            ],
            out_shape=shapes,
            input_output_aliases={5 + i: i for i in range(len(made))},
            compiler_params=params(),
            cost_estimate=cost(4 * part * rows * (head + 512), 4 * (part + rows) * head),
            name="pack_head",
        )(slot, value, front_in, pat_rows, after, *made)

    made = pack_head(0, piece, ())
    upper = plus(upper, lax.ppermute(upper, "row", TREE[0]), made[1])
    made = pack_head(2, upper, made)
    packed_head, keep, index = made
    upper = plus(upper, lax.ppermute(upper, "row", TREE[1]), keep)
    upper = plus(upper, lax.ppermute(upper, "row", TREE[2]))
    got_index = exchange(index[0].reshape(peers, CAP)).reshape(1, slots)

    send_head, low, lower = pl.pallas_call(
        update_kernel,
        grid=(4,),
        in_specs=[
            SMEM,
            whole((1, rows)),
            whole((sent, 2 * B)),
            inv_spec,
            whole((upper_rows, width)),
            head_spec,
            keep_spec,
        ],
        out_specs=[head_spec, low_spec, whole((rows, 2 * B))],
        out_shape=(
            jax.ShapeDtypeStruct((slots, head), BF),
            jax.ShapeDtypeStruct((slots, 2 * B), BF),
            jax.ShapeDtypeStruct((rows, 2 * B), BF),
        ),
        compiler_params=params(),
        cost_estimate=cost(4 * slots * B * (rows + head), 4 * slots * head),
        name="update_head",
    )(pos, slot, everything, upper_inv, upper, packed_head, keep)
    got_head = exchange(send_head.reshape(peers, CAP, head)).reshape(slots, head)
    packed_tail = pl.pallas_call(
        lambda *refs: pack_tail_kernel(head // B, *refs),
        grid=(4,),
        in_specs=[
            whole((1, rows)),
            pl.BlockSpec((1, rows, tail), lambda i: (0, 0, last)),
            keep_spec,
            ANY,
        ],
        out_specs=tail_spec,
        out_shape=jax.ShapeDtypeStruct((slots, tail), BF),
        compiler_params=params(),
        cost_estimate=cost(2 * slots * rows * (tail + 256), 2 * (slots + rows) * tail),
        name="pack_tail",
    )(slot, front_in, keep, send_head)
    send_tail = pl.pallas_call(
        lambda *refs: rest_kernel(head // B, *refs),
        grid=(4,),
        in_specs=[low_spec, pl.BlockSpec((2 * B, tail), lambda i: (0, last)), tail_spec, keep_spec],
        out_specs=tail_spec,
        out_shape=jax.ShapeDtypeStruct((slots, tail), BF),
        compiler_params=params(),
        cost_estimate=cost(4 * slots * B * tail, 8 * slots * tail),
        name="update_tail",
    )(low, upper, packed_tail, keep)
    got_tail = exchange(send_tail.reshape(peers, CAP, tail)).reshape(slots, tail)

    ancestor = pl.pallas_call(
        add_kernel,
        grid=(8,),
        in_specs=[whole((1, slots)), whole((slots, head))],
        out_specs=pl.BlockSpec((rows // 8, head), lambda i: (i, 0)),
        out_shape=jax.ShapeDtypeStruct((rows, width), F32),
        compiler_params=params(),
        cost_estimate=cost(2 * rows * slots * head, 4 * (rows + slots) * head),
        name="add_head",
    )(got_index, got_head)
    ancestor = pl.pallas_call(
        add_kernel,
        grid=(8,),
        in_specs=[whole((1, slots)), whole((slots, tail)), ANY],
        out_specs=pl.BlockSpec((rows // 8, tail), lambda i: (i, last)),
        out_shape=jax.ShapeDtypeStruct((rows, width), F32),
        input_output_aliases={2: 0},
        compiler_params=params(),
        cost_estimate=cost(4 * rows * slots * tail, 4 * (rows + slots) * tail),
        name="add_tail",
    )(got_index, got_tail, ancestor)
    return (lower[None], upper[None, : 2 * B], ancestor)


def solution(mesh):
    return jax.shard_map(
        local,
        mesh=mesh,
        in_specs=(
            P("gz", "row", "col"),
            P("gz", "row", "col"),
            P("gz", None, None, None),
            P("gz", None, None, None),
            P("gz", "row"),
        ),
        out_specs=(P("gz", "row", None), P("gz", None, "col"), P(("gz", "row"), "col")),
        check_vma=False,
    )
```

```python
import jax
import jax.numpy as jnp
from jax import lax
from jax.experimental import pallas as pl
from jax.experimental.pallas import tpu as pltpu
from jax.sharding import PartitionSpec as P

BF = jnp.bfloat16
F32 = jnp.float32
B = 256
CAP = 96
NOTE = 16
VMEM_LIMIT = 48 * 2**20


def params():
    return pltpu.CompilerParams(vmem_limit_bytes=VMEM_LIMIT)


def mm(a, b):
    return jnp.dot(a, b, preferred_element_type=F32)


def split(a):
    hi = a.astype(BF)
    return hi, (a - hi.astype(F32)).astype(BF)


def dot_split(a, b):
    ah, al = split(a)
    bh, bl = split(b)
    return mm(ah, bh) + (mm(ah, bl) + mm(al, bh))


def panels_zero_kernel(
    pos_ref, pat_ref, cols_ref, rows_ref, li_ref, ui_ref, send_ref, u_ref, corner_ref
):
    n_row, n_col = cols_ref.shape[1] // B, u_ref.shape[1] // B
    row0, col0 = pos_ref[0] * n_row, pos_ref[1] * n_col
    uh, ul = split(ui_ref[0, 0])
    lh, ll = split(li_ref[0, 0])
    for i in range(n_row):
        keep = jnp.where(row0 + i > 0, pat_ref[i, 0], 0).astype(F32)
        second = pat_ref[i, 1].astype(F32)
        block = cols_ref[0, i * B : (i + 1) * B, 0:B]
        base = i * (B + NOTE)
        send_ref[base : base + B, 0:B] = ((mm(block, uh) + mm(block, ul)) * keep).astype(BF)
        block = cols_ref[0, i * B : (i + 1) * B, B : 2 * B].astype(F32)
        send_ref[base : base + B, B : 2 * B] = (block * second).astype(BF)
        send_ref[base + B : base + B + NOTE, :] = (jnp.zeros((NOTE, 2 * B), F32) + second).astype(BF)
    for j in range(n_col):
        keep = jnp.where(col0 + j > 0, pat_ref[0, j], 0).astype(F32)
        block = rows_ref[0, 0:B, j * B : (j + 1) * B]
        u_ref[:, j * B : (j + 1) * B] = ((mm(lh, block) + mm(ll, block)) * keep).astype(BF)
    root = (pos_ref[1] == 0).astype(F32)
    corner_ref[0:B, :] = (send_ref[B + NOTE : 2 * B + NOTE, 0:B].astype(F32) * root).astype(BF)
    corner_ref[B : 2 * B, :] = (u_ref[:, B : 2 * B].astype(F32) * root).astype(BF)


def upper_kernel(pos_ref, pat_ref, rows_ref, li_ref, u0_ref, corner_ref, out_ref):
    n_col = u0_ref.shape[1] // B
    col0 = pos_ref[1] * n_col
    root = (pos_ref[0] == 0).astype(F32)
    out_ref[0:B, :] = (u0_ref[...].astype(F32) * root).astype(BF)
    n = B // n_col
    for j in range(n_col):
        keep = jnp.where(col0 + j > 1, pat_ref[1, j], 0).astype(F32)
        cols = slice(j * B, (j + 1) * B)
        block = rows_ref[0, B : 2 * B, cols].astype(F32) - mm(corner_ref[0:B, :], u0_ref[:, cols])
        out_ref[B : 2 * B, cols] = (dot_split(li_ref[0, 1], block) * (keep * root)).astype(BF)
        piece = corner_ref[B + j * n : B + (j + 1) * n, :].astype(F32)
        out_ref[2 * B : 2 * B + n, cols] = (piece * root).astype(BF)


def slots_kernel(pos_ref, targets_ref, slot_ref, value_ref):
    rows = targets_ref.shape[1]
    peers = 32
    target = targets_ref[...]
    peer = target // rows
    local = target - peer * rows
    row_id = pos_ref[0] * rows + lax.broadcasted_iota(jnp.int32, (1, rows), 1)
    valid = row_id >= 2 * B
    ids = lax.broadcasted_iota(jnp.int32, (peers, rows), 0)
    hot = jnp.where((ids == peer) & valid, 1.0, 0.0)
    before = jnp.where(
        lax.broadcasted_iota(jnp.int32, (B, B), 0) < lax.broadcasted_iota(jnp.int32, (B, B), 1), 1.0, 0.0
    ).astype(BF)
    seen = jnp.zeros((peers, 1), F32)
    for i in range(rows // B):
        part = hot[:, i * B : (i + 1) * B]
        rank = mm(part.astype(BF), before) + seen
        seen = seen + jnp.sum(part, axis=1, keepdims=True)
        place = rank + (CAP * ids[:, i * B : (i + 1) * B]).astype(F32)
        slot = jnp.sum(part * place, axis=0, keepdims=True).astype(jnp.int32)
        ok = valid[:, i * B : (i + 1) * B]
        slot_ref[:, i * B : (i + 1) * B] = jnp.where(ok, slot, -1)
    high = local // 64
    which = lax.broadcasted_iota(jnp.int32, (16, rows), 0)
    value = jnp.where(which == 0, high, jnp.where(which == 1, local - high * 64, jnp.where(which == 2, 1, 0)))
    value_ref[...] = value.astype(F32).astype(BF)


def one_hot(first, count, slot):
    ids = first + lax.broadcasted_iota(jnp.int32, (count, slot.shape[1]), 0)
    return jnp.where(ids == slot, 1.0, 0.0).astype(BF)


def pack_rows(first, hot, front_ref, keep, rows_ref):
    for j in range(rows_ref.shape[1] // B):
        cols = slice(j * B, (j + 1) * B)
        rows_ref[:, cols] = (mm(hot, front_ref[0, :, cols]) * keep[:, first + j : first + j + 1]).astype(BF)


def pack_head_kernel(first, slot_ref, value_ref, front_ref, pat_ref, *refs):
    rows_ref, keep_ref, index_ref = refs[-3:]
    count = rows_ref.shape[0]
    hot = one_hot((first + pl.program_id(0)) * count, count, slot_ref[...])
    keep = mm(hot, pat_ref[...])
    keep_ref[...] = keep.astype(BF)
    pack_rows(0, hot, front_ref, keep, rows_ref)
    info = lax.dot_general(value_ref[...], hot, (((1,), (1,)), ((), ())), preferred_element_type=F32)
    index = info[0:1] * 64.0 + info[1:2] + (1.0 - info[2:3]) * 4096.0
    index_ref[...] = jnp.broadcast_to(index, (8, count)).astype(jnp.int32)


def pack_tail_kernel(first, slot_ref, front_ref, keep_ref, after_ref, rows_ref):
    count = rows_ref.shape[0]
    hot = one_hot(pl.program_id(0) * count, count, slot_ref[...])
    pack_rows(first, hot, front_ref, keep_ref[...].astype(F32), rows_ref)


def subtract(out_ref, rows_ref, keep_ref, first, low, u_ref):
    for j in range(out_ref.shape[1] // B):
        cols = slice(j * B, (j + 1) * B)
        product = mm(low, u_ref[0 : 2 * B, cols])
        keep = keep_ref[:, first + j : first + j + 1].astype(F32)
        out_ref[:, cols] = (rows_ref[:, cols].astype(F32) - product * keep).astype(BF)


def update_kernel(
    pos_ref, slot_ref, all_ref, ui_ref, u_ref, rows_ref, keep_ref, out_ref, low_ref, lower_ref
):
    n_row = lower_ref.shape[0] // B
    n_col = u_ref.shape[1] // B

    @pl.when(pl.program_id(0) == 0)
    def _():
        corner = jnp.concatenate([u_ref[2 * B :, j * B : (j + 1) * B] for j in range(n_col)], axis=0)
        uh, ul = split(ui_ref[0, 1])
        for i in range(n_row):
            base, rows = i * (B + NOTE), slice(i * B, (i + 1) * B)
            low = all_ref[base : base + B, 0:B]
            keep = all_ref[base + B : base + B + NOTE, B : 2 * B].astype(F32)[0:1]
            keep = keep * (pos_ref[0] * n_row + i > 1).astype(F32)
            block = all_ref[base : base + B, B : 2 * B].astype(F32) - mm(low, corner)
            bh, bl = split(block)
            lower_ref[rows, 0:B] = low
            lower_ref[rows, B : 2 * B] = ((mm(bh, uh) + (mm(bh, ul) + mm(bl, uh))) * keep).astype(BF)

    count = rows_ref.shape[0]
    hot = one_hot(pl.program_id(0) * count, count, slot_ref[...])
    low = mm(hot, lower_ref[...]).astype(BF)
    low_ref[...] = low
    subtract(out_ref, rows_ref, keep_ref, 0, low, u_ref)


def rest_kernel(first, low_ref, u_ref, rows_ref, keep_ref, out_ref):
    subtract(out_ref, rows_ref, keep_ref, first, low_ref[...], u_ref)


def join_kernel(count, pos_ref, own_ref, *refs):
    piece_ref = refs[-1]
    piece = own_ref[...].astype(F32) * (pos_ref[1] == 0).astype(F32)
    for ref in refs[:count]:
        piece = piece + ref[...].astype(F32)
    piece_ref[...] = piece.astype(BF)


def add_kernel(index_ref, got_ref, *refs):
    out_ref = refs[-1]
    hot = one_hot(pl.program_id(0) * out_ref.shape[0], out_ref.shape[0], index_ref[...])
    out_ref[...] = mm(hot, got_ref[...])


def cost(flops, size):
    return pl.CostEstimate(flops=flops, bytes_accessed=size, transcendentals=0)


def whole(shape):
    return pl.BlockSpec(shape, lambda *_: (0,) * len(shape))


SMEM = pl.BlockSpec(memory_space=pltpu.SMEM)
ANY = pl.BlockSpec(memory_space=pl.ANY)
TREE = (((0, 4),), ((0, 2), (4, 6)), ((0, 1), (2, 3), (4, 5), (6, 7)))


def tree(block, axis):
    for pairs in TREE:
        block = block + lax.ppermute(block, axis, pairs)
    return block


def sum_kernel(a_ref, b_ref, *refs):
    refs[-1][...] = (a_ref[...].astype(F32) + b_ref[...].astype(F32)).astype(BF)


def plus(a, b, *after):
    return pl.pallas_call(
        sum_kernel,
        grid=(1,),
        in_specs=[whole(a.shape)] * 2 + [ANY] * len(after),
        out_specs=whole(a.shape),
        out_shape=jax.ShapeDtypeStruct(a.shape, a.dtype),
        compiler_params=params(),
        cost_estimate=cost(0, 6 * a.size),
        name="plus",
    )(a, b, *after)


def scatter(lower, axis, pos, *after):
    n = lax.axis_size(axis)
    rows = lower.shape[0] // n
    shape = (rows, lower.shape[1])
    got = [lax.ppermute(lower[c * rows : (c + 1) * rows], axis, [(0, c)]) for c in range(1, n)]
    return pl.pallas_call(
        lambda *refs: join_kernel(n - 1, *refs),
        grid=(1,),
        in_specs=[SMEM] + [whole(shape)] * n + [ANY] * len(after),
        out_specs=whole(shape),
        out_shape=jax.ShapeDtypeStruct(shape, lower.dtype),
        compiler_params=params(),
        cost_estimate=cost(0, 18 * rows * lower.shape[1]),
        name="join",
    )(pos, lower, *got, *after)


def local(front_in, pattern, lower_inv, upper_inv, targets):
    rows, width = front_in.shape[1:]
    n_row, n_col = rows // B, width // B
    peers = lax.axis_size("gz") * lax.axis_size("row")
    slots = peers * CAP
    pos = jnp.stack([lax.axis_index("row"), lax.axis_index("col")]).astype(jnp.int32)
    pat = pattern[0]
    part = slots // 4
    head = 3 * width // 4
    tail = width - head
    last = head // tail
    exchange = lambda x: lax.all_to_all(x, ("gz", "row"), split_axis=0, concat_axis=0, tiled=True)

    slot, value = pl.pallas_call(
        slots_kernel,
        in_specs=[SMEM, pl.BlockSpec(memory_space=pltpu.VMEM)],
        out_shape=(jax.ShapeDtypeStruct((1, rows), jnp.int32), jax.ShapeDtypeStruct((16, rows), BF)),
        cost_estimate=cost(10**9, 10**6),
        name="slots",
    )(pos, targets)

    cols_spec = pl.BlockSpec((1, rows, 2 * B), lambda *_: (0, 0, 0))
    rows_spec = pl.BlockSpec((1, 2 * B, width), lambda *_: (0, 0, 0))
    inv_spec = whole((1, 2, B, B))
    sent = n_row * (B + NOTE)
    upper_rows = 2 * B + B // n_col
    send, u0, corner = pl.pallas_call(
        panels_zero_kernel,
        grid=(1,),
        in_specs=[SMEM, SMEM, cols_spec, rows_spec, inv_spec, inv_spec],
        out_specs=[whole((sent, 2 * B)), whole((B, width)), whole((2 * B, B))],
        out_shape=(
            jax.ShapeDtypeStruct((sent, 2 * B), BF),
            jax.ShapeDtypeStruct((B, width), BF),
            jax.ShapeDtypeStruct((2 * B, B), BF),
        ),
        compiler_params=params(),
        cost_estimate=cost(4 * (rows + width) * B * B, 8 * (rows + width) * B),
        name="panels_zero",
    )(pos, pat, front_in, front_in, lower_inv, upper_inv)
    keep_col = (pos[1] * n_col + jnp.arange(n_col)) >= 2
    keep_pat = jnp.where(keep_col[None, :], pat, 0).astype(BF)
    pat_rows = jnp.pad(jnp.repeat(keep_pat, B, axis=0), ((0, 0), (0, 128 - n_col)))
    piece = scatter(send, "col", pos, slot, value, pat_rows)
    everything = lax.all_gather(piece, "col", axis=0, tiled=True)
    corner = tree(corner, "col")
    upper = pl.pallas_call(
        upper_kernel,
        grid=(1,),
        in_specs=[SMEM, SMEM, rows_spec, inv_spec, whole((B, width)), whole((2 * B, B))],
        out_specs=whole((upper_rows, width)),
        out_shape=jax.ShapeDtypeStruct((upper_rows, width), BF),
        compiler_params=params(),
        cost_estimate=cost(8 * width * B * B, 8 * width * B),
        name="upper",
    )(pos, pat, front_in, lower_inv, u0, corner)

    keep_spec = pl.BlockSpec((part, 128), lambda i: (i, 0))
    head_spec = pl.BlockSpec((part, head), lambda i: (i, 0))
    tail_spec = pl.BlockSpec((part, tail), lambda i: (i, 0))
    low_spec = pl.BlockSpec((part, 2 * B), lambda i: (i, 0))
    shapes = (
        jax.ShapeDtypeStruct((slots, head), BF),
        jax.ShapeDtypeStruct((slots, 128), BF),
        jax.ShapeDtypeStruct((8, slots), jnp.int32),
    )

    def pack_head(first, after, made):
        return pl.pallas_call(
            lambda *refs: pack_head_kernel(first, *refs),
            grid=(2,),
            in_specs=[
                whole((1, rows)),
                whole((16, rows)),
                pl.BlockSpec((1, rows, head), lambda i: (0, 0, 0)),
                whole((rows, 128)),
            ]
            + [ANY] * (1 + len(made)),
            out_specs=[
                pl.BlockSpec((part, head), lambda i: (first + i, 0)),
                pl.BlockSpec((part, 128), lambda i: (first + i, 0)),
                pl.BlockSpec((8, part), lambda i: (0, first + i)),
            ],
            out_shape=shapes,
            input_output_aliases={5 + i: i for i in range(len(made))},
            compiler_params=params(),
            cost_estimate=cost(4 * part * rows * (head + 512), 4 * (part + rows) * head),
            name="pack_head",
        )(slot, value, front_in, pat_rows, after, *made)

    made = pack_head(0, piece, ())
    upper = plus(upper, lax.ppermute(upper, "row", TREE[0]), made[1])
    made = pack_head(2, upper, made)
    packed_head, keep, index = made
    upper = plus(upper, lax.ppermute(upper, "row", TREE[1]), keep)
    upper = plus(upper, lax.ppermute(upper, "row", TREE[2]))
    got_index = exchange(index[0].reshape(peers, CAP)).reshape(1, slots)

    send_head, low, lower = pl.pallas_call(
        update_kernel,
        grid=(4,),
        in_specs=[
            SMEM,
            whole((1, rows)),
            whole((sent, 2 * B)),
            inv_spec,
            whole((upper_rows, width)),
            head_spec,
            keep_spec,
        ],
        out_specs=[head_spec, low_spec, whole((rows, 2 * B))],
        out_shape=(
            jax.ShapeDtypeStruct((slots, head), BF),
            jax.ShapeDtypeStruct((slots, 2 * B), BF),
            jax.ShapeDtypeStruct((rows, 2 * B), BF),
        ),
        compiler_params=params(),
        cost_estimate=cost(4 * slots * B * (rows + head), 4 * slots * head),
        name="update_head",
    )(pos, slot, everything, upper_inv, upper, packed_head, keep)
    got_head = exchange(send_head.reshape(peers, CAP, head)).reshape(slots, head)
    packed_tail = pl.pallas_call(
        lambda *refs: pack_tail_kernel(head // B, *refs),
        grid=(4,),
        in_specs=[
            whole((1, rows)),
            pl.BlockSpec((1, rows, tail), lambda i: (0, 0, last)),
            keep_spec,
            ANY,
        ],
        out_specs=tail_spec,
        out_shape=jax.ShapeDtypeStruct((slots, tail), BF),
        compiler_params=params(),
        cost_estimate=cost(2 * slots * rows * (tail + 256), 2 * (slots + rows) * tail),
        name="pack_tail",
    )(slot, front_in, keep, send_head)
    send_tail = pl.pallas_call(
        lambda *refs: rest_kernel(head // B, *refs),
        grid=(4,),
        in_specs=[low_spec, pl.BlockSpec((2 * B, tail), lambda i: (0, last)), tail_spec, keep_spec],
        out_specs=tail_spec,
        out_shape=jax.ShapeDtypeStruct((slots, tail), BF),
        compiler_params=params(),
        cost_estimate=cost(4 * slots * B * tail, 8 * slots * tail),
        name="update_tail",
    )(low, upper, packed_tail, keep)
    got_tail = exchange(send_tail.reshape(peers, CAP, tail)).reshape(slots, tail)

    ancestor = pl.pallas_call(
        add_kernel,
        grid=(8,),
        in_specs=[whole((1, slots)), whole((slots, head))],
        out_specs=pl.BlockSpec((rows // 8, head), lambda i: (i, 0)),
        out_shape=jax.ShapeDtypeStruct((rows, width), F32),
        compiler_params=params(),
        cost_estimate=cost(2 * rows * slots * head, 4 * (rows + slots) * head),
        name="add_head",
    )(got_index, got_head)
    ancestor = pl.pallas_call(
        add_kernel,
        grid=(8,),
        in_specs=[whole((1, slots)), whole((slots, tail)), ANY],
        out_specs=pl.BlockSpec((rows // 8, tail), lambda i: (i, last)),
        out_shape=jax.ShapeDtypeStruct((rows, width), F32),
        input_output_aliases={2: 0},
        compiler_params=params(),
        cost_estimate=cost(4 * rows * slots * tail, 4 * (rows + slots) * tail),
        name="add_tail",
    )(got_index, got_tail, ancestor)
    return (lower[None], upper[None, : 2 * B], ancestor)


def solution(mesh):
    return jax.shard_map(
        local,
        mesh=mesh,
        in_specs=(
            P("gz", "row", "col"),
            P("gz", "row", "col"),
            P("gz", None, None, None),
            P("gz", None, None, None),
            P("gz", "row"),
        ),
        out_specs=(P("gz", "row", None), P("gz", None, "col"), P(("gz", "row"), "col")),
        check_vma=False,
    )
```
